32 devices in a mesh: fsdp: 8 (over z, x), tensor: 4 (over y, core).
Axes of the slice: x: 2, y: 2, z: 4, core: 2. Of those that a mesh axis runs over, the one named last changes fastest.
Arguments:
- hidden: bfloat16 [128, 28672], P('tensor', 'fsdp'), may hold values from -6 to 6
- down_weight: bfloat16 [28672, 16384], P('fsdp', 'tensor'), may hold values from -0.03125 to 0.03125
- covariance: float32 [16384, 16384], P('tensor', 'fsdp'), as said below
- keep_index: int32 [8, 8], P('fsdp'), may hold values from -1 to 15, as said below
- start_basis: float32 [16384, 512], P('fsdp'), may hold values from -6 to 6
Outputs:
- mlp_out: bfloat16 [128, 16384], P('fsdp', 'tensor')
- new_covariance: float32 [16384, 16384], P('tensor', 'fsdp')
- first_basis: float32 [16384, 512], P(('tensor', 'fsdp'))
- final_basis: float32 [16384, 512], P('fsdp')
The draws below stay inside these ranges and needn't reach their ends.
Inputs may be any that keep to these rules, and one draw needn't show every extreme that they name: `keep_index`: row b lists first between 1 and 8 distinct positions of 0 to 15, then -1 in the remaining slots; in every draw some row lists 8 positions. covariance is exactly symmetric and positive definite.
All inputs are finite; a program needn't handle non-finite values.
Results may differ from the reference program's by a relative error of at most 0.0015.
Values may be sent and summed in bfloat16 or wider, within the bound.
No kernel may reach another device: no remote copies, remote signals or barrier semaphores. Data moves between devices by JAX's collectives and lax.ppermute only.
A program may use at most 192 MiB of HBM per device.

```python
import math
import jax
import jax.numpy as jnp
from jax import lax

D = 16384
FF = 28672
TOK_DEV = 16
RANK = 512
TOKENS = 128
KEEP_MOST = 8
N_TENSOR = 4


def draw_covariance(key, part):
    key_noise = jax.random.fold_in(key, 11)
    key_scale = jax.random.fold_in(key, 12)
    row_index = jnp.arange(D, dtype=jnp.float32)
    level = D / TOKENS
    spread = 0.9 * level / math.sqrt(D)
    roughness = jnp.exp(jax.random.uniform(key_scale, (D,), jnp.float32) * math.log(2.0))
    noise_field = jax.random.normal(key_noise, (D, D), jnp.float32) * spread
    symmetric = (noise_field + noise_field.T) * 0.5
    diagonal = level * (2.0 + 4.0 * row_index / D) * roughness
    return (symmetric + jnp.diag(diagonal)).astype(jnp.float32)


def draw_keep_index(key, part):
    key_order = jax.random.fold_in(key, 21)
    key_divisor = jax.random.fold_in(key, 22)
    key_trim = jax.random.fold_in(key, 23)
    key_full = jax.random.fold_in(key, 24)
    blocks = TOKENS // TOK_DEV
    scores = jax.random.randint(key_order, (blocks, TOK_DEV), 0, 1 << 20) * TOK_DEV + jnp.arange(TOK_DEV, dtype=jnp.int32)[None, :]
    ordering = jnp.argsort(scores, axis=1, stable=True)[:, :KEEP_MOST].astype(jnp.int32)
    divisor = 1 + jax.random.randint(key_divisor, (blocks,), 0, 4)
    trimmed = jax.random.randint(key_trim, (blocks,), 0, 2)
    counts = jnp.maximum(1, KEEP_MOST // divisor - trimmed)
    full_block = jax.random.randint(key_full, (), 0, blocks)
    counts = jnp.where(jnp.arange(blocks) == full_block, KEEP_MOST, counts)
    slot_index = jnp.arange(KEEP_MOST, dtype=jnp.int32)
    return jnp.where(slot_index[None, :] < counts[:, None], ordering, -1).astype(jnp.int32)


def raised(entries, stream_key, source, target, shards_of, factor):
    def block_of(dim):
        return (jnp.arange(entries.shape[dim]) // (entries.shape[dim] // shards_of)).reshape((-1,) + (1,) * (entries.ndim - 1 - dim))

    one_side = jax.random.permutation(stream_key, shards_of)[block_of(target)]
    second = (block_of(target) + shards_of // 2) % shards_of
    return jnp.where((block_of(source) == one_side) | (block_of(source) == second), factor * entries, entries)


def level_of(rng, dims, split, smallest, high):
    loudness = 1.0
    for axis_at, blocks in split:
        heights = jax.random.uniform(jax.random.fold_in(jax.random.fold_in(rng, 6), axis_at), (blocks,), jnp.float32, smallest / len(split), high / len(split))
        loudness = loudness * jnp.repeat(jnp.exp(heights), dims[axis_at] // blocks).reshape((-1,) + (1,) * (len(dims) - 1 - axis_at))
    return loudness


def noise(key, shape, deviation, bound, cuts=(), kind=jnp.bfloat16):
    drawn = deviation * jax.random.normal(key, shape, jnp.float32)
    if cuts:
        drawn = drawn * level_of(key, shape, cuts, -0.22, 0.18)
    return jnp.clip(drawn, -bound, bound).astype(kind)


def bell_draw_with(own_key, dims, scale, most, split, heavy, kind=jnp.bfloat16):
    values = scale * jax.random.normal(own_key, dims, jnp.float32)
    if split:
        values = values * level_of(own_key, dims, split, -0.22, 0.18)
    return jnp.clip(raised(values, jax.random.fold_in(own_key, 3), *heavy), -most, most).astype(kind)


def setup_inputs(seed: int = 0) -> dict:
    streams_of = jax.random.split(jax.random.key(seed), 6)
    hidden = bell_draw_with(streams_of[0], (TOKENS, FF), 1.0, 6.0, ((0, 4), (1, 8)), (1, 0, 8, 2.0))
    down_weight = noise(streams_of[1], (FF, D), FF ** -0.5, 0.03125, ((0, 8), (1, 4)))
    covariance = draw_covariance(jax.random.fold_in(streams_of[5], 71), 0)
    keep_index = draw_keep_index(jax.random.fold_in(streams_of[5], 71), 0)
    start_basis = noise(streams_of[4], (D, RANK), 1.0, 6.0, ((0, 8),), jnp.float32)
    return dict(hidden=hidden, down_weight=down_weight, covariance=covariance, keep_index=keep_index, start_basis=start_basis)


def orthonormal(image_rows):
    gram_matrix = jnp.dot(image_rows.T.astype(jnp.float32), image_rows.astype(jnp.float32), precision=lax.Precision.HIGHEST, preferred_element_type=jnp.float32)
    lower_factor = jnp.linalg.cholesky(gram_matrix)
    return jax.scipy.linalg.solve_triangular(lower_factor, image_rows.T, lower=True).T

def reference(hidden, down_weight, covariance, keep_index, start_basis):
    mlp_out = jnp.dot(hidden.astype(jnp.float32), down_weight.astype(jnp.float32), preferred_element_type=jnp.float32).astype(jnp.bfloat16)
    positions = jnp.arange(TOK_DEV, dtype=jnp.int32)
    keep_mask = jnp.any(keep_index[:, :, None] == positions[None, None, :], axis=1).reshape(TOKENS)
    kept_rows = mlp_out * keep_mask[:, None].astype(jnp.bfloat16)
    kept_blocks = kept_rows.reshape(TOKENS, N_TENSOR, D // N_TENSOR).transpose(1, 0, 2)
    cov_blocks = covariance.reshape(N_TENSOR, D // N_TENSOR, D)

    def update_block(pieces):
        cov_piece, kept_piece = pieces
        update = lax.dot_general(kept_piece.astype(jnp.float32), kept_rows.astype(jnp.float32), (((0,), (0,)), ((), ())), preferred_element_type=jnp.float32)
        return cov_piece + update * (1.0 / TOKENS)
    new_covariance = lax.map(update_block, (cov_blocks, kept_blocks)).reshape(D, D)
    image_one = jnp.dot(new_covariance.astype(jnp.float32), start_basis.astype(jnp.float32), precision=lax.Precision.HIGHEST, preferred_element_type=jnp.float32)
    basis_one = orthonormal(image_one)
    first_basis = basis_one * math.sqrt(D)
    image_two = jnp.dot(new_covariance.astype(jnp.float32), basis_one.astype(jnp.float32), precision=lax.Precision.HIGHEST, preferred_element_type=jnp.float32)
    final_basis = orthonormal(image_two) * math.sqrt(D)
    return (mlp_out, new_covariance, first_basis, final_basis)
```

```python
import math

import jax
import jax.numpy as jnp
from jax import lax
from jax.experimental import pallas as pl
from jax.experimental.pallas import tpu as pltpu
from jax.sharding import PartitionSpec as P

D = 16384
TOK_DEV = 16
HIGH = lax.Precision.HIGH
HIGHEST = lax.Precision.HIGHEST
NN = (((1,), (0,)), ((), ()))
NT = (((1,), (1,)), ((), ()))
TN = (((0,), (0,)), ((), ()))
PAD = 16
BLK = 128
TILE = 8


def base_factor(tiles_a, tiles_b, width):
    count = len(tiles_a)
    done_b = [[None] * TILE for _ in range(count)]
    for j in range(0, BLK, width):
        group, first = divmod(j, TILE)
        rows_a = [jnp.broadcast_to(tiles_a[group][first + a : first + a + 1, :], (TILE, BLK)) for a in range(width)]
        rows_b = [jnp.broadcast_to(tiles_b[group][first + a : first + a + 1, :], (TILE, BLK)) for a in range(width)]
        pivot = [[None] * width for _ in range(width)]
        for a in range(width):
            for b in range(a, width):
                pivot[a][b] = jnp.broadcast_to(rows_a[a][:, j + b : j + b + 1], (TILE, BLK))
        inverse = [None] * width
        for a in range(width):
            inverse[a] = 1.0 / pivot[a][a]
            for b in range(a + 1, width):
                factor = pivot[a][b] * inverse[a]
                for c in range(b, width):
                    pivot[b][c] = pivot[b][c] - factor * pivot[a][c]
                rows_a[b] = rows_a[b] - factor * rows_a[a]
                rows_b[b] = rows_b[b] - factor * rows_b[a]
        for a in range(width):
            done_b[group][first + a] = rows_b[a][0:1, :] * lax.rsqrt(pivot[a][a])[0:1, :]
        if j + width >= BLK:
            break
        solved_a, solved_b = [None] * width, [None] * width
        for a in reversed(range(width)):
            left, right = rows_a[a], rows_b[a]
            for b in range(a + 1, width):
                left = left - pivot[a][b] * solved_a[b]
                right = right - pivot[a][b] * solved_b[b]
            solved_a[a], solved_b[a] = left * inverse[a], right * inverse[a]
        for g in range((j + width) // TILE, count):
            left, right = tiles_a[g], tiles_b[g]
            for a in range(width):
                column = jnp.broadcast_to(tiles_a[g][:, j + a : j + a + 1], (TILE, BLK))
                left = left - column * solved_a[a]
                right = right - column * solved_b[a]
            tiles_a[g], tiles_b[g] = left, right
    return [jnp.concatenate(rows, axis=0) for rows in done_b]


def inverse_factor_kernel(gram_ref, out_ref, work, base):
    size = gram_ref.shape[0]
    blocks = size // BLK
    row = lax.broadcasted_iota(jnp.int32, (size, size), 0)
    col = lax.broadcasted_iota(jnp.int32, (size, size), 1)
    work[:, 0:size] = gram_ref[...]
    work[:, size:] = jnp.where(row == col, 1.0, 0.0)
    lane = lax.broadcasted_iota(jnp.int32, (TILE, BLK), 1)
    sub = lax.broadcasted_iota(jnp.int32, (TILE, BLK), 0)
    for k in range(blocks):
        lo, hi = k * BLK, (k + 1) * BLK
        tiles_a = [work[lo + g * TILE : lo + (g + 1) * TILE, lo:hi] for g in range(BLK // TILE)]
        tiles_b = [jnp.where(lane == sub + g * TILE, 1.0, 0.0) for g in range(BLK // TILE)]
        for g, tile in enumerate(base_factor(tiles_a, tiles_b, 4)):
            base[g * TILE : (g + 1) * TILE, :] = tile
        unit = base[...]
        if k + 1 < blocks:
            right = jnp.dot(unit, work[lo:hi, hi:size], precision=HIGHEST, preferred_element_type=jnp.float32)
        left = jnp.dot(unit, work[lo:hi, size : size + hi], precision=HIGHEST, preferred_element_type=jnp.float32)
        out_ref[lo:hi, 0:hi] = left
        if k + 1 < blocks:
            out_ref[lo:hi, hi:size] = jnp.zeros((BLK, size - hi), jnp.float32)
            tn = (((0,), (0,)), ((), ()))
            work[hi:size, hi:size] -= lax.dot_general(right, right, tn, precision=HIGHEST, preferred_element_type=jnp.float32)
            work[hi:size, size : size + hi] -= lax.dot_general(right, left, tn, precision=HIGHEST, preferred_element_type=jnp.float32)


def inverse_factor(gram):
    size = gram.shape[0]
    return pl.pallas_call(
        inverse_factor_kernel,
        out_shape=jax.ShapeDtypeStruct((size, size), jnp.float32),
        scratch_shapes=[pltpu.VMEM((size, 2 * size), jnp.float32), pltpu.VMEM((BLK, BLK), jnp.float32)],
        compiler_params=pltpu.CompilerParams(vmem_limit_bytes=16 * 1024 * 1024),
        name="inverse_factor",
    )(gram)


def dot(left, right, dims=NN, precision=HIGH):
    return lax.dot_general(left, right, dims, precision=precision, preferred_element_type=jnp.float32)


def swap(x, axis, bit):
    return lax.ppermute(x, axis, [(i, i ^ bit) for i in range(lax.axis_size(axis))])


def bits_of(axis):
    return [1 << b for b in range(lax.axis_size(axis).bit_length() - 1)]


def pack(x):
    top = jnp.max(jnp.abs(x))
    power = jnp.where(top > 0, jnp.ceil(jnp.log2(top)), 0.0)
    power = jnp.maximum(power, -100.0) - 15.0
    values = (x * jnp.exp2(-power)).astype(jnp.float16)
    return jnp.concatenate([values, jnp.full((PAD, x.shape[1]), power, jnp.float16)], axis=0)


def unpack(message):
    rows = message.shape[0] - PAD
    power = message[rows, 0].astype(jnp.float32)
    return message[:rows].astype(jnp.float32) * jnp.exp2(power)


def block(x, index, size, axis):
    return lax.dynamic_slice_in_dim(x, index * size, size, axis)


def gather_relative(x, axis, bits):
    held = {0: x}
    for bit in bits:
        for m in sorted(held):
            held[m ^ bit] = swap(held[m], axis, bit)
    return held


def gather_rows(x, axis, bits):
    held, order = x[None], [0]
    for bit in bits:
        held = jnp.concatenate([held, swap(held, axis, bit)], axis=0)
        order = order + [m ^ bit for m in order]
    place = sorted(range(len(order)), key=lambda i: order[i])
    return jnp.stack([held[i] for i in place])


def sum_rows(x, axis, bits, relative):
    for bit in bits:
        other = swap(x, axis, bit)
        if relative:
            other = jnp.stack([other[m ^ bit] for m in range(x.shape[0])])
        x = x + other
    return x


def sum_square(x):
    f_bits, t_bits = bits_of("fsdp"), bits_of("tensor")
    halved = [("tensor", bit) for bit in t_bits] + [("fsdp", bit) for bit in f_bits[:1]]
    for axis, bit in halved:
        half = x.shape[0] // 2
        side = (lax.axis_index(axis) & bit) // bit
        x = block(x, side, half, 0) + swap(block(x, 1 - side, half, 0), axis, bit)
    for bit in f_bits[1:]:
        x = x + swap(x, "fsdp", bit)
    for axis, bit in reversed(halved):
        other = swap(x, axis, bit)
        side = (lax.axis_index(axis) & bit) // bit
        x = jnp.where(side == 0, jnp.concatenate([x, other]), jnp.concatenate([other, x]))
    return x


def scatter_tokens(partial, bits, row_of):
    held = {m: row_of(partial, m) for m in range(lax.axis_size("fsdp"))}
    for bit in bits:
        sent = [m for m in sorted(held) if m & bit]
        came = swap(jnp.stack([held[m] for m in sent]), "fsdp", bit)
        for at, m in enumerate(sent):
            held[m ^ bit] = held[m ^ bit] + came[at]
            del held[m]
    return held[0]


def body(hidden, down_weight, covariance, keep_index, start_basis):
    f_count, t_count = lax.axis_size("fsdp"), lax.axis_size("tensor")
    f, t = lax.axis_index("fsdp"), lax.axis_index("tensor")
    f_bits, t_bits = bits_of("fsdp"), bits_of("tensor")
    quarter, width = covariance.shape
    rank = start_basis.shape[1]
    share = quarter // f_count
    group = f_count // t_count
    part = width // t_count
    root = math.sqrt(D)

    tokens = gather_rows(hidden, "tensor", t_bits[::-1])
    tokens = tokens.reshape(-1, hidden.shape[1])
    partial_out = jnp.dot(tokens, down_weight, preferred_element_type=jnp.float32)

    def token_rows(x, m):
        owner = f ^ m
        return block(x, ((owner // group) ^ t) * group + owner % group, TOK_DEV, 0)

    half = partial_out.shape[1] // 2
    swapped = f_bits[1:2] + f_bits[:1] + f_bits[2:]
    mlp_out = jnp.concatenate(
        [
            scatter_tokens(partial_out[:, :half], f_bits, token_rows),
            scatter_tokens(partial_out[:, half:], swapped, token_rows),
        ],
        axis=1,
    ).astype(jnp.bfloat16)

    positions = jnp.arange(TOK_DEV, dtype=jnp.int32)
    picks = (keep_index[0][:, None] == positions[None, :]).astype(jnp.bfloat16)
    kept = jnp.dot(picks, mlp_out, preferred_element_type=jnp.float32).astype(jnp.bfloat16)
    slots = kept.shape[0]
    row_data = gather_rows(kept, "fsdp", f_bits[::-1])
    column_data = block(row_data, f % group, width, 2) * (t == f // group).astype(jnp.bfloat16)
    for bit in t_bits:
        column_data = column_data + swap(column_data, "tensor", bit)
    row_data = row_data.reshape(f_count * slots, quarter)
    column_flat = column_data.reshape(f_count * slots, width)
    per_token = 1.0 / (TOK_DEV * f_count)

    held = {}
    for m in sorted(range(f_count), key=lambda m: (-(m & 1), -m)):
        held[m] = dot(block(covariance, f ^ m, share, 0), start_basis)
    for bit in f_bits:
        for m in sorted((m for m in held if m & bit), key=lambda m: -m):
            came = unpack(swap(pack(held.pop(m)), "fsdp", bit))
            held[m ^ bit] = held[m ^ bit] + came
    raw = held[0].T

    kept_start = dot(column_flat.astype(jnp.float32), start_basis).reshape(f_count, slots, rank)
    kept_start = sum_rows(kept_start, "fsdp", f_bits, True).reshape(f_count * slots, rank) * per_token

    def kept_part(m):
        return dot(kept_start, block(row_data, f ^ m, share, 1).astype(jnp.float32), TN)

    own = raw + kept_part(0)
    pieces = gather_relative(pack(raw), "fsdp", f_bits[::-1])

    total = dot(own, block(covariance, f, share, 0))
    for m in range(1, f_count):
        image = unpack(pieces[m]) + kept_part(m)
        total = total + dot(image, block(covariance, f ^ m, share, 0))
    seconds = {m: block(total, t ^ m, part, 1) for m in range(t_count)}
    for at, bit in enumerate(t_bits):
        for m in sorted((m for m in seconds if m & bit), key=lambda m: -m):
            sent = seconds.pop(m)
            came = swap(sent, "tensor", bit) if at == 0 else unpack(swap(pack(sent), "tensor", bit))
            seconds[m ^ bit] = seconds[m ^ bit] + came
    kept_image = dot(block(row_data, f, share, 1).astype(jnp.float32), own, NT)
    kept_image = kept_image.reshape(f_count, slots, rank)
    kept_image = sum_rows(kept_image, "tensor", t_bits, False)
    kept_image = sum_rows(kept_image, "fsdp", f_bits, True).reshape(f_count * slots, rank) * per_token
    second = seconds[0] + dot(kept_image, block(column_flat, t, part, 1).astype(jnp.float32), TN)

    first_inverse = inverse_factor(sum_square(dot(own, own, NT, HIGHEST)))
    first_basis = lax.dot_general(
        own, first_inverse, (((0,), (1,)), ((), ())), precision=HIGH, preferred_element_type=jnp.float32
    ) * root

    second = dot(first_inverse, second)
    last_inverse = inverse_factor(sum_square(dot(second, second, NT, HIGHEST)))
    parts = gather_rows(second.T, "tensor", t_bits[::-1])
    image = jnp.concatenate([lax.dynamic_index_in_dim(parts, t ^ m, 0, False) for m in range(t_count)])
    final_basis = dot(image, last_inverse, NT) * root

    update = lax.dot_general(row_data, column_flat, TN, preferred_element_type=jnp.float32)
    new_covariance = covariance + update * per_token
    return (mlp_out, new_covariance, first_basis, final_basis)


def solution(mesh):
    placed = (
        P("tensor", "fsdp"),
        P("fsdp", "tensor"),
        P("tensor", "fsdp"),
        P("fsdp", None),
        P("fsdp", None),
    )
    return jax.shard_map(
        body,
        mesh=mesh,
        in_specs=placed,
        out_specs=(
            P("fsdp", "tensor"),
            P("tensor", "fsdp"),
            P(("tensor", "fsdp"), None),
            P("fsdp", None),
        ),
        check_vma=False,
    )
```

```python
import math

import jax
import jax.numpy as jnp
from jax import lax
from jax.experimental import pallas as pl
from jax.experimental.pallas import tpu as pltpu
from jax.sharding import PartitionSpec as P

D = 16384
TOK_DEV = 16
HIGH = lax.Precision.HIGH
HIGHEST = lax.Precision.HIGHEST
NN = (((1,), (0,)), ((), ()))
NT = (((1,), (1,)), ((), ()))
TN = (((0,), (0,)), ((), ()))

BLK = 128
TILE = 8


def base_factor(tiles_a, tiles_b, width):
    count = len(tiles_a)
    done_b = [[None] * TILE for _ in range(count)]
    for j in range(0, BLK, width):
        group, first = divmod(j, TILE)
        rows_a = [jnp.broadcast_to(tiles_a[group][first + a : first + a + 1, :], (TILE, BLK)) for a in range(width)]
        rows_b = [jnp.broadcast_to(tiles_b[group][first + a : first + a + 1, :], (TILE, BLK)) for a in range(width)]
        pivot = [[None] * width for _ in range(width)]
        for a in range(width):
            for b in range(a, width):
                pivot[a][b] = jnp.broadcast_to(rows_a[a][:, j + b : j + b + 1], (TILE, BLK))
        inverse = [None] * width
        for a in range(width):
            inverse[a] = 1.0 / pivot[a][a]
            for b in range(a + 1, width):
                factor = pivot[a][b] * inverse[a]
                for c in range(b, width):
                    pivot[b][c] = pivot[b][c] - factor * pivot[a][c]
                rows_a[b] = rows_a[b] - factor * rows_a[a]
                rows_b[b] = rows_b[b] - factor * rows_b[a]
        for a in range(width):
            done_b[group][first + a] = rows_b[a][0:1, :] * lax.rsqrt(pivot[a][a])[0:1, :]
        if j + width >= BLK:
            break
        solved_a, solved_b = [None] * width, [None] * width
        for a in reversed(range(width)):
            left, right = rows_a[a], rows_b[a]
            for b in range(a + 1, width):
                left = left - pivot[a][b] * solved_a[b]
                right = right - pivot[a][b] * solved_b[b]
            solved_a[a], solved_b[a] = left * inverse[a], right * inverse[a]
        for g in range((j + width) // TILE, count):
            left, right = tiles_a[g], tiles_b[g]
            for a in range(width):
                column = jnp.broadcast_to(tiles_a[g][:, j + a : j + a + 1], (TILE, BLK))
                left = left - column * solved_a[a]
                right = right - column * solved_b[a]
            tiles_a[g], tiles_b[g] = left, right
    return [jnp.concatenate(rows, axis=0) for rows in done_b]


def inverse_factor_kernel(gram_ref, out_ref, work, base):
    size = gram_ref.shape[0]
    blocks = size // BLK
    row = lax.broadcasted_iota(jnp.int32, (size, size), 0)
    col = lax.broadcasted_iota(jnp.int32, (size, size), 1)
    work[:, 0:size] = gram_ref[...]
    work[:, size:] = jnp.where(row == col, 1.0, 0.0)
    lane = lax.broadcasted_iota(jnp.int32, (TILE, BLK), 1)
    sub = lax.broadcasted_iota(jnp.int32, (TILE, BLK), 0)
    for k in range(blocks):
        lo, hi = k * BLK, (k + 1) * BLK
        tiles_a = [work[lo + g * TILE : lo + (g + 1) * TILE, lo:hi] for g in range(BLK // TILE)]
        tiles_b = [jnp.where(lane == sub + g * TILE, 1.0, 0.0) for g in range(BLK // TILE)]
        for g, tile in enumerate(base_factor(tiles_a, tiles_b, TILE)):
            base[g * TILE : (g + 1) * TILE, :] = tile
        unit = base[...]
        if k + 1 < blocks:
            right = jnp.dot(unit, work[lo:hi, hi:size], precision=HIGHEST, preferred_element_type=jnp.float32)
        left = jnp.dot(unit, work[lo:hi, size : size + hi], precision=HIGHEST, preferred_element_type=jnp.float32)
        out_ref[lo:hi, 0:hi] = left
        if k + 1 < blocks:
            out_ref[lo:hi, hi:size] = jnp.zeros((BLK, size - hi), jnp.float32)
            tn = (((0,), (0,)), ((), ()))
            work[hi:size, hi:size] -= lax.dot_general(right, right, tn, precision=HIGHEST, preferred_element_type=jnp.float32)
            work[hi:size, size : size + hi] -= lax.dot_general(right, left, tn, precision=HIGHEST, preferred_element_type=jnp.float32)


def inverse_factor(gram):
    size = gram.shape[0]
    return pl.pallas_call(
        inverse_factor_kernel,
        out_shape=jax.ShapeDtypeStruct((size, size), jnp.float32),
        scratch_shapes=[pltpu.VMEM((size, 2 * size), jnp.float32), pltpu.VMEM((BLK, BLK), jnp.float32)],
        compiler_params=pltpu.CompilerParams(vmem_limit_bytes=16 * 1024 * 1024),
        name="inverse_factor",
    )(gram)


def split(x):
    high = x.astype(jnp.bfloat16)
    return high, (x - high.astype(jnp.float32)).astype(jnp.bfloat16)


def mxu(left, right, dims=NN):
    return lax.dot_general(left, right, dims, preferred_element_type=jnp.float32)


def rows_kernel(ids_ref, cov_ref, start_ref, out_ref, top_ref, high, low):
    first = (pl.program_id(0) == 0) & (pl.program_id(1) == 0)

    @pl.when(first)
    def _():
        high[...], low[...] = split(start_ref[...])
        top_ref[...] = jnp.zeros_like(top_ref)

    cov_high, cov_low = split(cov_ref[...])
    image = mxu(cov_high, high[...]) + (mxu(cov_low, high[...]) + mxu(cov_high, low[...]))
    out_ref[0] = image.T
    top_ref[...] = jnp.maximum(top_ref[...], jnp.max(jnp.abs(image), axis=0, keepdims=True))


def rows_times(covariance, start_basis, ids, share):
    width, rank = start_basis.shape
    count = ids.shape[0]
    tall = min(share, 256)
    steps = share // tall
    return pl.pallas_call(
        rows_kernel,
        grid_spec=pltpu.PrefetchScalarGridSpec(
            num_scalar_prefetch=1,
            grid=(count, steps),
            in_specs=[
                pl.BlockSpec((tall, width), lambda p, i, ids_ref: (ids_ref[p] * steps + i, 0)),
                pl.BlockSpec((width, rank), lambda p, i, ids_ref: (0, 0)),
            ],
            out_specs=[
                pl.BlockSpec((1, rank, tall), lambda p, i, ids_ref: (p, 0, i)),
                pl.BlockSpec((8, rank), lambda p, i, ids_ref: (0, 0)),
            ],
            scratch_shapes=[pltpu.VMEM((width, rank), jnp.bfloat16)] * 2,
        ),
        out_shape=[
            jax.ShapeDtypeStruct((count, rank, share), jnp.float32),
            jax.ShapeDtypeStruct((8, rank), jnp.float32),
        ],
        compiler_params=pltpu.CompilerParams(vmem_limit_bytes=40 * 1024 * 1024),
        cost_estimate=pl.CostEstimate(
            flops=6 * count * share * width * rank,
            bytes_accessed=4 * count * share * (width + rank),
            transcendentals=0,
        ),
        name="rows_times",
    )(ids, covariance, start_basis)


def update_kernel(count, rank, per_token, first, ids_ref, cov_ref, row_ref, column_ref, *rest):
    pieces, (out_ref, total_ref, high, low) = rest[:count], rest[-4:]
    p, i = pl.program_id(0), pl.program_id(1)
    kept = row_ref[...]
    steps, _, tall = high.shape

    for k in range(count):

        @pl.when((p == k) & (i == 0))
        def _():
            piece_high, piece_low = split(pieces[k][...])
            for s in range(steps):
                high[s, :rank, :] = piece_high[:, s * tall : (s + 1) * tall]
                low[s] = piece_low[:, s * tall : (s + 1) * tall]

    @pl.when((p == 0) & (i == 0))
    def _():
        total_ref[...] = jnp.zeros_like(total_ref) if first else rest[count][...]

    high[i, rank:, :] = kept
    cov = cov_ref[...]
    out_ref[...] = cov + mxu(kept, column_ref[...], TN) * per_token
    cov_high, cov_low = split(cov)
    total_ref[...] += mxu(high[i], cov_high) + mxu(high[i], cov_low)
    total_ref[:rank, :] += mxu(low[i], cov_high)


def update_and_multiply(covariance, row_data, column_data, pieces, ids, before, updated, per_token):
    count = len(pieces)
    rank, share = pieces[0].shape
    tokens, width = column_data.shape
    tall = min(share, 256)
    steps = share // tall
    high_rows = rank + tokens
    first = before is None

    def fixed(shape):
        return pl.BlockSpec(shape, lambda p, i, ids_ref: (0, 0))

    rows = pl.BlockSpec((tall, width), lambda p, i, ids_ref: (ids_ref[p] * steps + i, 0))
    operands = [covariance, row_data, column_data, *pieces]
    in_specs = [
        rows,
        pl.BlockSpec((tokens, tall), lambda p, i, ids_ref: (0, ids_ref[p] * steps + i)),
        fixed((tokens, width)),
        *[fixed((rank, share))] * count,
    ]
    aliases = {}
    if not first:
        operands += [before, updated]
        in_specs += [fixed((high_rows, width)), pl.BlockSpec(memory_space=pl.ANY)]
        aliases = {len(operands): 0}
    return pl.pallas_call(
        lambda *refs: update_kernel(count, rank, per_token, first, *refs),
        grid_spec=pltpu.PrefetchScalarGridSpec(
            num_scalar_prefetch=1,
            grid=(count, steps),
            in_specs=in_specs,
            out_specs=[rows, fixed((high_rows, width))],
            scratch_shapes=[
                pltpu.VMEM((steps, high_rows, tall), jnp.bfloat16),
                pltpu.VMEM((steps, rank, tall), jnp.bfloat16),
            ],
        ),
        out_shape=[
            jax.ShapeDtypeStruct(covariance.shape, jnp.float32),
            jax.ShapeDtypeStruct((high_rows, width), jnp.float32),
        ],
        input_output_aliases=aliases,
        compiler_params=pltpu.CompilerParams(vmem_limit_bytes=48 * 1024 * 1024),
        cost_estimate=pl.CostEstimate(
            flops=6 * count * share * width * rank,
            bytes_accessed=8 * count * share * width,
            transcendentals=0,
        ),
        name="update_and_multiply",
    )(ids, *operands)


def basis_kernel(scale, ids_ref, factor_ref, image_ref, out_ref):
    factor_high, factor_low = split(factor_ref[...])
    image_high, image_low = split(image_ref[0])
    basis = mxu(factor_high, image_high) + (mxu(factor_high, image_low) + mxu(factor_low, image_high))
    out_ref[...] = basis.T * scale


def basis_of(factor, images, ids, scale):
    count, rank, part = images.shape
    return pl.pallas_call(
        lambda *refs: basis_kernel(scale, *refs),
        grid_spec=pltpu.PrefetchScalarGridSpec(
            num_scalar_prefetch=1,
            grid=(count,),
            in_specs=[
                pl.BlockSpec((rank, rank), lambda p, ids_ref: (0, 0)),
                pl.BlockSpec((1, rank, part), lambda p, ids_ref: (ids_ref[p], 0, 0)),
            ],
            out_specs=pl.BlockSpec((part, rank), lambda p, ids_ref: (p, 0)),
        ),
        out_shape=jax.ShapeDtypeStruct((count * part, rank), jnp.float32),
        compiler_params=pltpu.CompilerParams(vmem_limit_bytes=32 * 1024 * 1024),
        cost_estimate=pl.CostEstimate(
            flops=6 * count * part * rank * rank, bytes_accessed=8 * count * part * rank, transcendentals=0
        ),
        name="basis_of",
    )(ids, factor, images)


def dot(left, right, dims=NN, precision=HIGH):
    return lax.dot_general(left, right, dims, precision=precision, preferred_element_type=jnp.float32)


def swap(x, axis, bit):
    return lax.ppermute(x, axis, [(i, i ^ bit) for i in range(lax.axis_size(axis))])


def bits_of(axis):
    return [1 << b for b in range(lax.axis_size(axis).bit_length() - 1)]


def power_over(top):
    exponent = jnp.where(top > 0, jnp.ceil(jnp.log2(top)), 0.0)
    return jnp.full((8, 128), jnp.maximum(exponent, -90.0), jnp.float32)


def pack(x, power):
    return (x * jnp.exp2(15.0 - power[0, 0])).astype(jnp.float16)


def unpack(message, power):
    return message.astype(jnp.float32) * jnp.exp2(power[0, 0] - 15.0)


def block(x, index, size, axis):
    return lax.dynamic_slice_in_dim(x, index * size, size, axis)


def gather_relative(x, axis, bits):
    held = {0: x}
    for bit in bits:
        for m in sorted(held):
            held[m ^ bit] = swap(held[m], axis, bit)
    return held


def gather_rows(x, axis, bits):
    for bit in bits:
        x = jnp.concatenate([x, swap(x, axis, bit)], axis=0)
    return x


def mirror(m, axis):
    bits = bits_of(axis)
    return sum(((m // bit) & 1) * other for bit, other in zip(bits, bits[::-1]))


def sum_whole(x, axes):
    for axis in axes:
        for bit in bits_of(axis)[::-1]:
            x = x + swap(x, axis, bit)
    return x


def side_of(axis, bit):
    return (lax.axis_index(axis) & bit) // bit


def sum_halves(x, axis):
    for bit in bits_of(axis):
        half, side = x.shape[0] // 2, side_of(axis, bit)
        x = block(x, side, half, 0) + swap(block(x, 1 - side, half, 0), axis, bit)
    return x


def join_halves(x, axis):
    for bit in bits_of(axis)[::-1]:
        other = swap(x, axis, bit)
        x = jnp.where(side_of(axis, bit) == 0, jnp.concatenate([x, other]), jnp.concatenate([other, x]))
    return x


def tie(*values):
    return lax.optimization_barrier(values)


def scatter_step(held, bit):
    leaving = [m for m in sorted(held) if m & bit]
    return jnp.stack([held.pop(m) for m in leaving]), leaving


def scatter_add(held, came, leaving, bit):
    for at, m in enumerate(leaving):
        held[m ^ bit] = held[m ^ bit] + came[at]


def body(hidden, down_weight, covariance, keep_index, start_basis):
    f_count, t_count = lax.axis_size("fsdp"), lax.axis_size("tensor")
    f, t = lax.axis_index("fsdp"), lax.axis_index("tensor")
    f_bits, t_bits = bits_of("fsdp"), bits_of("tensor")
    quarter, width = covariance.shape
    rank = start_basis.shape[1]
    share = quarter // f_count
    group = f_count // t_count
    part = width // t_count
    root = math.sqrt(D)
    per_token = 1.0 / (TOK_DEV * f_count)

    tokens = gather_rows(hidden, "tensor", t_bits[::-1])
    leaving = sorted((m for m in range(f_count) if m & 1), key=lambda m: (-(m & 2), -m))
    staying = sorted((m for m in range(f_count) if not m & 1), reverse=True)
    sent, top_sent = rows_times(covariance, start_basis, f ^ jnp.array(leaving, jnp.int32), share)
    power_sent = power_over(jnp.max(top_sent))
    power_came = swap(power_sent, "fsdp", 1)
    per_message = len(leaving) // 2
    tokens, power_came, message, message_later = tie(
        tokens, power_came, pack(sent[:per_message], power_sent), pack(sent[per_message:], power_sent)
    )

    partial_out = jnp.dot(tokens, down_weight, preferred_element_type=jnp.float32)
    came_early = swap(message, "fsdp", 1)
    came_early, partial_out, message_later = tie(came_early, partial_out, message_later)

    def token_rows(x, m):
        owner = f ^ m
        place = mirror((owner // group) ^ t, "tensor")
        return block(x, place * group + owner % group, TOK_DEV, 0)

    half = partial_out.shape[1] // 2
    orders = (f_bits[1:] + f_bits[:1], f_bits[:0:-1] + f_bits[:1])
    token_sums = [{m: token_rows(partial_out[:, at : at + half], m) for m in range(f_count)} for at in (0, half)]

    def token_step(step):
        return [scatter_step(held, order[step]) for held, order in zip(token_sums, orders)]

    def token_add(step, left, came):
        for held, order, (_, gone), arrived in zip(token_sums, orders, left, came):
            scatter_add(held, arrived, gone, order[step])

    def token_swap(step, messages):
        return [swap(message, "fsdp", order[step]) for message, order in zip(messages, orders)]

    left = token_step(0)
    start_later, message_later, *messages = tie(start_basis, message_later, *[message for message, _ in left])

    came_late = swap(message_later, "fsdp", 1)
    came = token_swap(0, messages)
    stayed, top_stayed = rows_times(covariance, start_later, f ^ jnp.array(staying, jnp.int32), share)
    came_late, stayed, top_stayed, *came = tie(came_late, stayed, top_stayed, *came)
    token_add(0, left, came)
    power = jnp.maximum(power_over(jnp.maximum(jnp.max(top_sent), jnp.max(top_stayed))), power_came)
    powers = []
    for bit in f_bits[1:]:
        power = jnp.maximum(power, swap(power, "fsdp", bit))
        powers.append(power + (len(powers) + 1))
    held = {m: stayed[i] for i, m in enumerate(staying)}
    scatter_add(held, unpack(came_early, power_came), leaving[:per_message], 1)
    scatter_add(held, unpack(came_late, power_came), leaving[per_message:], 1)

    power, *powers = tie(power, *powers)
    for step in range(1, len(f_bits)):
        image, gone = scatter_step(held, f_bits[step])
        left = token_step(step)
        image, *messages = tie(pack(image, powers[step - 1]), *[message for message, _ in left])
        came = token_swap(step, messages)
        image_came = swap(image, "fsdp", f_bits[step])
        if step == 1:
            power_other = swap(power, "fsdp", 1)
            image_came, power_other, *came = tie(image_came, power_other, *came)
            power = jnp.maximum(power, power_other) + len(f_bits)
        elif step + 1 < len(f_bits):
            image_came, *came = tie(image_came, *came)
        token_add(step, left, came)
        if step + 1 < len(f_bits):
            scatter_add(held, unpack(image_came, powers[step - 1]), gone, f_bits[step])
    mlp_out = jnp.concatenate([held_rows[0] for held_rows in token_sums], axis=1).astype(jnp.bfloat16)

    positions = jnp.arange(TOK_DEV, dtype=jnp.int32)
    picks = (keep_index[0][:, None] == positions[None, :]).astype(jnp.bfloat16)
    row_data = jnp.dot(picks, mlp_out, preferred_element_type=jnp.float32).astype(jnp.bfloat16)
    slots = row_data.shape[0]
    order = jnp.arange(f_count * slots, dtype=jnp.int32)
    source = mirror((order // slots) ^ f, "fsdp") * slots + order % slots
    arrange = (source[:, None] == order[None, :]).astype(jnp.bfloat16)
    row_data = gather_rows(row_data, "fsdp", f_bits[:1:-1])
    row_data, image_came = tie(row_data, image_came)
    scatter_add(held, unpack(image_came, powers[-1]), gone, f_bits[-1])
    raw = held[0]

    pieces = {0: pack(raw, power)}

    def gather_stage(weight):
        chosen = [m for m in range(f_count) if m.bit_count() == weight]
        return {m: swap(pieces[m & (m - 1)], "fsdp", m & -m) for m in chosen}

    def settle(stage, *others):
        done = tie(*stage.values(), *others)
        pieces.update(zip(stage, done))
        return done[len(stage) :]

    row_data, pieces[0] = tie(gather_rows(row_data, "fsdp", f_bits[1:2]), pieces[0])
    stage = gather_stage(1)
    row_data = gather_rows(row_data, "fsdp", f_bits[:1])
    row_data = jnp.dot(arrange, row_data, preferred_element_type=jnp.float32).astype(jnp.bfloat16)
    gram_part = sum_halves(dot(raw, raw, NT, HIGHEST), "tensor")
    row_data, gram_part = settle(stage, row_data, gram_part)
    own_rows = block(row_data, f, share, 1).astype(jnp.float32)
    for weight in range(2, len(f_bits)):
        stage = gather_stage(weight)
        if weight == 2:
            column_data = block(row_data, f % group, width, 1) * (t == f // group).astype(jnp.bfloat16)
            column_data = sum_whole(column_data, ["tensor"])
            both = jnp.concatenate([raw, own_rows], axis=0)
            products = sum_whole(dot(own_rows, both, NT), ["tensor"])
            kept_start = dot(column_data.astype(jnp.float32), start_basis)
            column_data, products, kept_start = settle(stage, column_data, products, kept_start)
        else:
            settle(stage)

    def small_step(bit, values):
        return [swap(value, "fsdp", bit) for value in values]

    small = [kept_start, products, gram_part]
    for bit in f_bits[:2:-1]:
        small = [a + b for a, b in zip(small, tie(*small_step(bit, small)))]
    stage = gather_stage(len(f_bits))
    came = small_step(f_bits[2], small)
    total = new_covariance = None
    for odd in (0, 1):
        chosen = [m for m in range(f_count) if m & 1 == odd]
        new_covariance, total = update_and_multiply(
            covariance,
            row_data,
            column_data,
            [raw if m == 0 else unpack(pieces[m], power) for m in chosen],
            f ^ jnp.array(chosen, jnp.int32),
            total,
            new_covariance,
            per_token,
        )
        if odd == 0:
            total, new_covariance, *came = settle(stage, total, new_covariance, *came)
            small = [a + b for a, b in zip(small, came)]
            came = small_step(f_bits[1], small)
        else:
            total, new_covariance, *came = tie(total, new_covariance, *came)
            small = [a + b for a, b in zip(small, came)]
    seconds = {m: block(total, t ^ m, part, 1) for m in range(t_count)}
    came = small_step(1, small)
    for at, bit in enumerate(t_bits):
        leave, gone = scatter_step(seconds, bit)
        if at == 0:
            arrived = swap(leave, "tensor", bit)
            arrived, *came = tie(arrived, *came)
            kept_start, products, gram_part = [a + b for a, b in zip(small, came)]
            kept_start = kept_start * per_token
            raw_gram = join_halves(gram_part, "tensor")
            kept_raw, kept_square = products[:, :rank], products[:, rank:]
            kept_image = kept_raw + dot(kept_square, kept_start)
            middle = dot(kept_start, (kept_raw + kept_image) * 0.5, TN)
            first_gram = raw_gram + middle + middle.T
        else:
            images, kept = leave[:, :rank], leave[:, rank:]
            power_left = power_over(jnp.max(jnp.abs(images)))
            power_other = swap(power_left, "tensor", bit)
            message, power_other, kept, first_gram = tie(pack(images, power_left), power_other, kept, first_gram)
            arrived = [swap(message, "tensor", bit), swap(kept, "tensor", bit)]
            if at == 1:
                first_inverse = inverse_factor(first_gram)
                *arrived, first_inverse = tie(*arrived, first_inverse)
            arrived = jnp.concatenate([unpack(arrived[0], power_other), arrived[1]], axis=1)
        scatter_add(seconds, arrived, gone, bit)
    second = (
        seconds[0][:rank]
        + dot(kept_start, seconds[0][rank:], TN)
        + dot(kept_image, block(column_data, t, part, 1).astype(jnp.float32) * per_token, TN)
    )

    second = dot(first_inverse, second)
    second, last_gram = tie(second, sum_halves(dot(second, second, NT, HIGHEST), "tensor"))
    arrived = swap(second, "tensor", t_bits[-1])
    for bit in f_bits[::-1]:
        last_gram = last_gram + swap(last_gram, "fsdp", bit)
    arrived, last_gram = tie(arrived, last_gram)
    last_gram = join_halves(last_gram, "tensor")
    parts = gather_rows(jnp.stack([second, arrived]), "tensor", t_bits[-2::-1])
    own = raw + dot(kept_start, own_rows, TN)
    first_basis = lax.dot_general(
        own, first_inverse, (((0,), (1,)), ((), ())), precision=HIGH, preferred_element_type=jnp.float32
    ) * root
    last_gram, parts, first_basis = tie(last_gram, parts, first_basis)
    last_inverse = inverse_factor(last_gram)
    places = jnp.stack([mirror(t ^ m, "tensor") for m in range(t_count)])
    final_basis = basis_of(last_inverse, parts, places, root)
    return (mlp_out, new_covariance, first_basis, final_basis)


def solution(mesh):
    placed = (
        P("tensor", "fsdp"),
        P("fsdp", "tensor"),
        P("tensor", "fsdp"),
        P("fsdp", None),
        P("fsdp", None),
    )
    return jax.shard_map(
        body,
        mesh=mesh,
        in_specs=placed,
        out_specs=(
            P("fsdp", "tensor"),
            P("tensor", "fsdp"),
            P(("tensor", "fsdp"), None),
            P("fsdp", None),
        ),
        check_vma=False,
    )
```
